32 devices in a mesh: replica: 8 (over y, x, core), shard: 4 (over z).
Axes of the slice: x: 2, y: 2, z: 4, core: 2. Of those that a mesh axis runs over, the one named last changes fastest.
Arguments:
- tokens: bfloat16 [4096, 960], P(('replica', 'shard')), may hold values from -6 to 6
- seq_lengths: int32 [32, 3], P(('replica', 'shard')), may hold values from 1 to 64, 128 in all within a row
- norm_one: bfloat16 [960], P('shard'), may hold values from 0.099609375 to 1.8984375
- query_weight: bfloat16 [960, 960], P('shard'), may hold values from -0.1875 to 0.1875
- key_weight: bfloat16 [960, 320], P('shard'), may hold values from -0.1875 to 0.1875
- value_weight: bfloat16 [960, 320], P('shard'), may hold values from -0.1875 to 0.1875
- output_weight: bfloat16 [960, 960], P('shard'), may hold values from -0.75 to 0.75
- norm_two: bfloat16 [960], P('shard'), may hold values from 0.099609375 to 1.8984375
- gate_weight: bfloat16 [960, 2560], P('shard'), may hold values from -0.1875 to 0.1875
- up_weight: bfloat16 [960, 2560], P('shard'), may hold values from -0.1875 to 0.1875
- down_weight: bfloat16 [2560, 960], P('shard'), may hold values from -0.125 to 0.125
- out_grad: bfloat16 [4096, 960], P(('replica', 'shard')), may hold values from -6 to 6
Outputs:
- mixed: bfloat16 [4096, 960], P(('replica', 'shard'))
- input_grad: float32 [4096, 960], P(('replica', 'shard'))
- norm_one_grad: float32 [960], P('shard')
- query_grad: float32 [960, 960], P('shard')
- key_grad: float32 [960, 320], P('shard')
- value_grad: float32 [960, 320], P('shard')
- output_grad: float32 [960, 960], P('shard')
- norm_two_grad: float32 [960], P('shard')
- gate_grad: float32 [960, 2560], P('shard')
- up_grad: float32 [960, 2560], P('shard')
- down_grad: float32 [2560, 960], P('shard')
The draws below stay inside these ranges and needn't reach their ends.
Inputs may be any that keep to these rules, and one draw needn't show every extreme that they name: `seq_lengths`: each device's row sums to 128, and its longest sequence has exactly 64 tokens.
All inputs are finite; a program needn't handle non-finite values.
Results may differ from the reference program's by a relative error of at most 0.013.
Values may be sent and summed in bfloat16 or wider, within the bound.
A program may use at most 128 MiB of HBM per device.

```python
import math
import jax
import jax.numpy as jnp
import numpy as np
from jax import lax

D = 960
HEADS = 15
KV_HEADS = 5
HEAD = 64
FF = 2560
TOK_DEV = 128
PACK = 3
KV = 320
TOKENS = 4096
N_REPLICA = 8
N_SHARD = 4


def level_of(key, dims, split, smallest, top_value):
    loudness = 1.0
    for axis_at, blocks in split:
        steps = jax.random.uniform(jax.random.fold_in(jax.random.fold_in(key, 6), axis_at), (blocks,), jnp.float32, smallest / len(split), top_value / len(split))
        loudness = loudness * jnp.repeat(jnp.exp(steps), dims[axis_at] // blocks).reshape((-1,) + (1,) * (len(dims) - 1 - axis_at))
    return loudness


def profile(count, total, most, slope):
    portions = [(1 << 20) // math.isqrt(grade ** slope) + 1 for grade in range(2, count + 1)]
    surplus, counts = total - most - (count - 1), [1] * (count - 1)
    while surplus > 0:
        movable = [i for i in range(count - 1) if counts[i] < most]
        pool, remaining = sum([portions[i] for i in movable]), surplus
        for i in movable:
            more = min(most - counts[i], max(1, remaining * portions[i] // pool), surplus)
            counts[i] = counts[i] + more
            surplus = surplus - more
    return np.array([most] + counts)


def ragged_sizes(own_key, count, total, bound, lean):
    if count == 2:
        one = jax.random.randint(own_key, (), max(1, total - bound), min(bound, total - 1) + 1)
        return jnp.stack([one, total - one])
    tallies = jnp.asarray(profile(count, total, bound, lean), jnp.int32)
    twos = (count - 1) // 2
    giver, receiver = tallies[1:1 + 2 * twos:2], tallies[2:2 + 2 * twos:2]
    room = jnp.minimum(giver - 1, bound - receiver)
    moved = jax.random.randint(jax.random.fold_in(own_key, 1), (twos,), 0, 1 << 20) % (room + 1)
    tallies = tallies.at[1:1 + 2 * twos:2].set(giver - moved).at[2:2 + 2 * twos:2].set(receiver + moved)
    return tallies[jax.random.permutation(jax.random.fold_in(own_key, 2), count)]


def noise(stream_key, shape, scale, bound, shards=(), kind=jnp.bfloat16):
    values = scale * jax.random.normal(stream_key, shape, jnp.float32)
    if shards:
        values = values * level_of(stream_key, shape, shards, -0.22, 0.18)
    return jnp.clip(values, -bound, bound).astype(kind)


def setup_inputs(seed: int = 0) -> dict:
    arg_keys = jax.random.split(jax.random.key(seed), 13)
    return {
        "tokens": noise(arg_keys[0], (TOKENS, D), 1.0, 6.0, ((0, 32),)),
        "seq_lengths": jax.vmap(lambda own: ragged_sizes(own, PACK, TOK_DEV, TOK_DEV // 2, 2))(jax.random.split(arg_keys[1], (N_REPLICA * N_SHARD))).reshape((N_REPLICA * N_SHARD, PACK)).astype(jnp.int32),
        "norm_one": jnp.clip(1.0 + 0.18 * jax.random.normal(arg_keys[2], (D,), jnp.float32), 0.099609375, 1.8984375).astype(jnp.bfloat16),
        "query_weight": noise(arg_keys[3], (D, D), D ** -0.5, 0.1875, ((0, 4),)),
        "key_weight": noise(arg_keys[4], (D, KV), D ** -0.5, 0.1875, ((0, 4),)),
        "value_weight": noise(arg_keys[5], (D, KV), D ** -0.5, 0.1875, ((0, 4),)),
        "output_weight": noise(arg_keys[6], (D, D), (D // 16) ** -0.5, 0.75, ((0, 4),)),
        "norm_two": jnp.clip(1.0 + 0.18 * jax.random.normal(arg_keys[7], (D,), jnp.float32), 0.099609375, 1.8984375).astype(jnp.bfloat16),
        "gate_weight": noise(arg_keys[8], (D, FF), D ** -0.5, 0.1875, ((0, 4),)),
        "up_weight": noise(arg_keys[9], (D, FF), D ** -0.5, 0.1875, ((0, 4),)),
        "down_weight": noise(arg_keys[10], (FF, D), FF ** -0.5, 0.125, ((0, 4),)),
        "out_grad": noise(arg_keys[11], (TOKENS, D), 1.0, 6.0, ((0, 32),)),
    }


EPSILON = 1e-05
THETA = 100000.0

@jax.custom_vjp
def low(v):
    return lax.optimization_barrier(v.astype(jnp.bfloat16)).astype(jnp.float32)

@jax.custom_vjp
def low_back(v):
    return v

def low_keep(v):
    return (low(v), None)

def low_pass(kept, grad):
    return (grad,)

def back_keep(v):
    return (v, None)

def back_low(kept, grad):
    return (low(grad),)
low.defvjp(low_keep, low_pass)
low_back.defvjp(back_keep, back_low)

def layout(length_row, count):
    index_row = jnp.arange(count, dtype=jnp.int32)
    seq_ends = jnp.cumsum(length_row).astype(jnp.int32)
    seq_starts = seq_ends - length_row.astype(jnp.int32)
    doc_index = lax.optimization_barrier(jnp.sum((index_row[:, None] >= seq_ends[None, :]).astype(jnp.int32), axis=1))
    one_hot = doc_index[:, None] == jnp.arange(length_row.shape[0], dtype=jnp.int32)[None, :]
    first_slot = lax.optimization_barrier(jnp.sum(jnp.where(one_hot, seq_starts[None, :], 0), axis=1)).astype(jnp.int32)
    return (doc_index, index_row - first_slot)

def tables(positions, head_size):
    half_size = head_size // 2
    freq_index = jnp.arange(half_size, dtype=jnp.float32)
    inverse = THETA ** (-2.0 * freq_index / head_size)
    angles = positions.astype(jnp.float32)[..., None] * inverse
    return (jnp.cos(angles), jnp.sin(angles))

def rotate(values, cosine, sine):
    half_size = values.shape[-1] // 2
    first_half = values[..., :half_size]
    second_half = values[..., half_size:]
    cos_heads = cosine[..., None, :]
    sin_heads = sine[..., None, :]
    return jnp.concatenate([first_half * cos_heads - second_half * sin_heads, second_half * cos_heads + first_half * sin_heads], axis=-1)

def project(left, right):
    return jnp.einsum('gtd,de->gte', left, right, precision=lax.Precision.HIGHEST)

def block_forward(hidden_in, params, cosine, sine, allowed):
    norm_one, query_weight, key_weight, value_weight, output_weight, norm_two, gate_weight, up_weight, down_weight = params
    highest = lax.Precision.HIGHEST
    groups, count, width = hidden_in.shape
    group_heads = HEADS // KV_HEADS
    score_scale = 1.0 / math.sqrt(HEAD)
    scale_one = lax.rsqrt(lax.optimization_barrier(jnp.mean(hidden_in * hidden_in, axis=-1, keepdims=True)) + EPSILON)
    normed_one = low(hidden_in * scale_one * norm_one)
    queries_pre = low_back(project(normed_one, query_weight)).reshape(groups, count, HEADS, HEAD)
    query_rot = low(rotate(queries_pre, cosine, sine)).reshape(groups, count, KV_HEADS, group_heads, HEAD)
    keys_pre = low_back(project(normed_one, key_weight)).reshape(groups, count, KV_HEADS, HEAD)
    key_rot = low(rotate(keys_pre, cosine, sine))
    value_rot = low(low_back(project(normed_one, value_weight))).reshape(groups, count, KV_HEADS, HEAD)
    raw_scores = jnp.einsum('gtkhd,gskd->gkhts', query_rot, key_rot, precision=highest)
    scores = jnp.where(allowed[:, None, None, :, :], low_back(raw_scores) * score_scale, -1e+30)
    probs_low = low(jax.nn.softmax(scores, axis=-1))
    context = jnp.einsum('gkhts,gskd->gtkhd', probs_low, value_rot, precision=highest).reshape(groups, count, width)
    context = low_back(low(context))
    after_attn = hidden_in + low_back(project(context, output_weight))
    scale_two = lax.rsqrt(lax.optimization_barrier(jnp.mean(after_attn * after_attn, axis=-1, keepdims=True)) + EPSILON)
    normed_two = low(after_attn * scale_two * norm_two)
    gate_pre = low_back(project(normed_two, gate_weight))
    up_pre = low_back(project(normed_two, up_weight))
    act = low(jax.nn.silu(gate_pre) * up_pre)
    return after_attn + low_back(project(act, down_weight))

def reference(tokens, seq_lengths, norm_one, query_weight, key_weight, value_weight, output_weight, norm_two, gate_weight, up_weight, down_weight, out_grad):
    devices = N_REPLICA * N_SHARD
    doc_index, positions = jax.vmap(lambda length_row: layout(length_row, TOK_DEV))(seq_lengths)
    cosine, sine = tables(positions, HEAD)
    slots = jnp.arange(TOK_DEV, dtype=jnp.int32)
    causal = slots[:, None] >= slots[None, :]
    allowed = (doc_index[:, :, None] == doc_index[:, None, :]) & causal[None]
    params = tuple((weight.astype(jnp.float32) for weight in (norm_one, query_weight, key_weight, value_weight, output_weight, norm_two, gate_weight, up_weight, down_weight)))
    limit = max(1, 4096 // TOK_DEV)
    group = max((candidate for candidate in range(1, limit + 1) if devices % candidate == 0))
    steps = devices // group
    inputs = tokens.astype(jnp.float32).reshape(steps, group, TOK_DEV, D)
    cotangents = out_grad.astype(jnp.float32).reshape(steps, group, TOK_DEV, D)
    half_size = HEAD // 2
    cos_blocks = cosine.reshape(steps, group, TOK_DEV, half_size)
    sin_blocks = sine.reshape(steps, group, TOK_DEV, half_size)
    mask_blocks = allowed.reshape(steps, group, TOK_DEV, TOK_DEV)

    def one_step(totals, block):
        hidden_in, cotangent, cos_block, sin_block, mask_block = block

        def forward(hidden_x, weights):
            return block_forward(hidden_x, weights, cos_block, sin_block, mask_block)
        result, pullback = jax.vjp(forward, hidden_in, params)
        input_part, weight_grads = pullback(cotangent)
        totals = jax.tree.map(lambda left, right: left + right, totals, weight_grads)
        return (totals, (result, input_part))
    zeros = tuple((jnp.zeros_like(weight) for weight in params))
    totals, (results, input_parts) = lax.scan(one_step, zeros, (inputs, cotangents, cos_blocks, sin_blocks, mask_blocks))
    mixed = results.reshape(TOKENS, D).astype(jnp.bfloat16)
    input_grad = input_parts.reshape(TOKENS, D).astype(jnp.float32)
    return (mixed, input_grad, totals[0], totals[1], totals[2], totals[3], totals[4], totals[5], totals[6], totals[7], totals[8])
```

```python
import math

import jax
import jax.numpy as jnp
from jax import lax
from jax.sharding import PartitionSpec as P

HEADS = 15
KV_HEADS = 5
HEAD = 64


EPSILON = 1e-05
THETA = 100000.0


def layout(length_row, count):
    index_row = jnp.arange(count, dtype=jnp.int32)
    seq_ends = jnp.cumsum(length_row)
    seq_starts = seq_ends - length_row
    doc_index = jnp.sum((index_row[:, None] >= seq_ends[None, :]).astype(jnp.int32), axis=1)
    one_hot = doc_index[:, None] == jnp.arange(length_row.shape[0], dtype=jnp.int32)[None, :]
    first_slot = jnp.sum(jnp.where(one_hot, seq_starts[None, :], 0), axis=1)
    return (doc_index, index_row - first_slot)


def tables(positions, head_size):
    half_size = head_size // 2
    freq_index = jnp.arange(half_size, dtype=jnp.float32)
    inverse = THETA ** (-2.0 * freq_index / head_size)
    angles = positions.astype(jnp.float32)[..., None] * inverse
    return (jnp.cos(angles), jnp.sin(angles))


def rotate(values, cosine, sine):
    half_size = values.shape[-1] // 2
    first_half = values[..., :half_size]
    second_half = values[..., half_size:]
    cos_heads = cosine[:, None, :]
    sin_heads = sine[:, None, :]
    return jnp.concatenate(
        [
            first_half * cos_heads - second_half * sin_heads,
            second_half * cos_heads + first_half * sin_heads,
        ],
        axis=-1,
    )


def unrotate(grads, cosine, sine):
    half_size = grads.shape[-1] // 2
    first_half = grads[..., :half_size]
    second_half = grads[..., half_size:]
    cos_heads = cosine[:, None, :]
    sin_heads = sine[:, None, :]
    return jnp.concatenate(
        [
            first_half * cos_heads + second_half * sin_heads,
            second_half * cos_heads - first_half * sin_heads,
        ],
        axis=-1,
    )


def matmul(left, right):
    return jnp.dot(left, right, preferred_element_type=jnp.float32)


def matmul_right_t(left, right):
    return jnp.einsum("te,de->td", left, right, preferred_element_type=jnp.float32)


def matmul_left_t(left, right):
    return jnp.einsum("td,te->de", left, right, preferred_element_type=jnp.float32)


def masked_scores(query_rot, key_rot, allowed, score_scale):
    raw_scores = jnp.einsum(
        "tkhd,skd->khts", query_rot, key_rot, preferred_element_type=jnp.float32
    )
    return jnp.where(allowed[None, None], raw_scores * score_scale, -1e30)


def gather_weights(*shards):
    return tuple(lax.all_gather(shard, "shard", axis=0, tiled=True) for shard in shards)


def weight_grads(
    normed_one, context, normed_two, out_grad, qkv_back, attn_low, gate_back, up_back, act
):
    n_replica = lax.axis_size("replica")
    n_shard = lax.axis_size("shard")
    count, width = normed_one.shape
    ff = act.shape[1]
    kv_width = KV_HEADS * HEAD

    def over_copies(rows):
        return lax.all_gather(rows, "replica", axis=0, tiled=True)

    def parts(columns):
        return columns.reshape(count, n_replica, -1)

    act_parts = act.reshape(count, n_shard, n_replica, -1).swapaxes(1, 2)
    columns = jnp.concatenate(
        [
            parts(gate_back),
            parts(up_back),
            act_parts.reshape(count, n_replica, -1),
            parts(qkv_back),
            parts(attn_low),
        ],
        axis=2,
    )
    columns = lax.all_to_all(columns, "replica", split_axis=1, concat_axis=0, tiled=True)
    columns = columns.reshape(n_replica * count, -1)
    ff_part = ff // n_replica
    qkv_part = qkv_back.shape[1] // n_replica
    out_part = width // n_replica
    cuts = [0, 2 * ff_part, 3 * ff_part, 3 * ff_part + qkv_part, columns.shape[1]]
    gate_up, act_cols, qkv_cols, out_cols = (
        columns[:, low:high] for low, high in zip(cuts[:-1], cuts[1:])
    )
    row_part = jnp.concatenate(
        [
            matmul_left_t(over_copies(normed_two), gate_up),
            matmul_left_t(over_copies(normed_one), qkv_cols),
            matmul_left_t(over_copies(context), out_cols),
        ],
        axis=1,
    ).astype(jnp.bfloat16)
    down_part = matmul_left_t(act_cols, over_copies(out_grad)).astype(jnp.bfloat16)
    own_rows = width // n_shard
    down_rows = ff_part // n_shard
    row_terms = lax.all_to_all(
        row_part.reshape(n_shard, own_rows, -1), "shard", split_axis=0, concat_axis=0, tiled=True
    )
    down_terms = lax.all_to_all(
        down_part.reshape(n_shard, down_rows, width),
        "shard",
        split_axis=0,
        concat_axis=0,
        tiled=True,
    )
    row_own = jnp.sum(row_terms.astype(jnp.float32), axis=0).astype(jnp.bfloat16)
    down_own = jnp.sum(down_terms.astype(jnp.float32), axis=0).astype(jnp.bfloat16)
    row_all = lax.all_gather(row_own, "replica", axis=0)
    down_all = lax.all_gather(down_own, "replica", axis=0, tiled=True)

    def whole(low, high):
        piece = row_all[:, :, low:high].swapaxes(0, 1).astype(jnp.float32)
        return piece.reshape(own_rows, -1)

    qkv_grad = whole(2 * ff_part, 2 * ff_part + qkv_part)
    return (
        qkv_grad[:, :width],
        qkv_grad[:, width : width + kv_width],
        qkv_grad[:, width + kv_width :],
        whole(2 * ff_part + qkv_part, 2 * ff_part + qkv_part + out_part),
        whole(0, ff_part),
        whole(ff_part, 2 * ff_part),
        down_all.astype(jnp.float32),
    )


def on_device(
    tokens,
    seq_lengths,
    norm_one,
    query_weight,
    key_weight,
    value_weight,
    output_weight,
    norm_two,
    gate_weight,
    up_weight,
    down_weight,
    out_grad,
):
    count, width = tokens.shape
    group_heads = HEADS // KV_HEADS
    score_scale = 1.0 / math.sqrt(HEAD)
    doc_index, positions = layout(seq_lengths[0], count)
    cosine, sine = tables(positions, HEAD)
    slots = jnp.arange(count, dtype=jnp.int32)
    allowed = (doc_index[:, None] == doc_index[None, :]) & (slots[:, None] >= slots[None, :])
    gain_one, gain_two, wide_qkv, wide_output, wide_gate, wide_up, wide_down = gather_weights(
        norm_one,
        norm_two,
        jnp.concatenate([query_weight, key_weight, value_weight], axis=1),
        output_weight,
        gate_weight,
        up_weight,
        down_weight,
    )
    hidden_in = tokens.astype(jnp.float32)
    scale_one = lax.rsqrt(jnp.mean(hidden_in * hidden_in, axis=-1, keepdims=True) + EPSILON)
    normed_one = (hidden_in * scale_one * gain_one.astype(jnp.float32)).astype(jnp.bfloat16)
    qkv_pre = matmul(normed_one, wide_qkv)
    kv_width = KV_HEADS * HEAD
    queries_pre = qkv_pre[:, :width].reshape(count, HEADS, HEAD)
    query_rot = (
        rotate(queries_pre, cosine, sine)
        .astype(jnp.bfloat16)
        .reshape(count, KV_HEADS, group_heads, HEAD)
    )
    keys_pre = qkv_pre[:, width : width + kv_width].reshape(count, KV_HEADS, HEAD)
    key_rot = rotate(keys_pre, cosine, sine).astype(jnp.bfloat16)
    value_rot = qkv_pre[:, width + kv_width :].astype(jnp.bfloat16).reshape(count, KV_HEADS, HEAD)
    scores = masked_scores(query_rot, key_rot, allowed, score_scale)
    log_total = jax.nn.logsumexp(scores, axis=-1, keepdims=True)
    probs_low = jnp.exp(scores - log_total).astype(jnp.bfloat16)
    context = jnp.einsum("khts,skd->tkhd", probs_low, value_rot, preferred_element_type=jnp.float32)
    context = context.reshape(count, width).astype(jnp.bfloat16)
    after_attn = hidden_in + matmul(context, wide_output)
    scale_two = lax.rsqrt(jnp.mean(after_attn * after_attn, axis=-1, keepdims=True) + EPSILON)
    normed_two = (after_attn * scale_two * gain_two.astype(jnp.float32)).astype(jnp.bfloat16)
    gate_pre = matmul(normed_two, wide_gate)
    up_pre = matmul(normed_two, wide_up)
    sigmoid_gate = jax.nn.sigmoid(gate_pre)
    silu_gate = gate_pre * sigmoid_gate
    act = (silu_gate * up_pre).astype(jnp.bfloat16)
    mixed = (after_attn + matmul(act, wide_down)).astype(jnp.bfloat16)
    cotangent = out_grad.astype(jnp.float32)
    act_grad = matmul_right_t(out_grad, wide_down)
    gate_back = (act_grad * up_pre * sigmoid_gate * (1.0 + gate_pre * (1.0 - sigmoid_gate))).astype(
        jnp.bfloat16
    )
    up_back = (act_grad * silu_gate).astype(jnp.bfloat16)
    normed_two_grad = matmul_right_t(gate_back, wide_gate) + matmul_right_t(up_back, wide_up)
    gain_two_sum = jnp.sum(normed_two_grad * after_attn * scale_two, axis=0)
    weighted_two = normed_two_grad * gain_two.astype(jnp.float32)
    attn_out_grad = (
        cotangent
        + scale_two * weighted_two
        - after_attn * scale_two**3 * jnp.mean(after_attn * weighted_two, axis=-1, keepdims=True)
    )
    attn_low = attn_out_grad.astype(jnp.bfloat16)
    context_grad = (
        matmul_right_t(attn_low, wide_output)
        .astype(jnp.bfloat16)
        .reshape(count, KV_HEADS, group_heads, HEAD)
    )
    scores = masked_scores(query_rot, key_rot, allowed, score_scale)
    probs = jnp.exp(scores - log_total)
    probs_low = probs.astype(jnp.bfloat16)
    value_back = jnp.einsum(
        "khts,tkhd->skd", probs_low, context_grad, preferred_element_type=jnp.float32
    )
    value_back = value_back.reshape(count, KV_HEADS * HEAD).astype(jnp.bfloat16)
    probs_grad = jnp.einsum(
        "tkhd,skd->khts", context_grad, value_rot, preferred_element_type=jnp.float32
    )
    row_inner = jnp.sum(probs * probs_grad, axis=-1, keepdims=True)
    score_back = (probs * (probs_grad - row_inner) * score_scale).astype(jnp.bfloat16)
    query_rot_grad = jnp.einsum(
        "khts,skd->tkhd", score_back, key_rot, preferred_element_type=jnp.float32
    )
    key_rot_grad = jnp.einsum(
        "khts,tkhd->skd", score_back, query_rot, preferred_element_type=jnp.float32
    )
    query_back = (
        unrotate(query_rot_grad.reshape(count, HEADS, HEAD), cosine, sine)
        .reshape(count, width)
        .astype(jnp.bfloat16)
    )
    key_back = (
        unrotate(key_rot_grad, cosine, sine).reshape(count, KV_HEADS * HEAD).astype(jnp.bfloat16)
    )
    qkv_back = jnp.concatenate([query_back, key_back, value_back], axis=1)
    normed_one_grad = matmul_right_t(qkv_back, wide_qkv)
    gain_one_sum = jnp.sum(normed_one_grad * hidden_in * scale_one, axis=0)
    weighted_one = normed_one_grad * gain_one.astype(jnp.float32)
    input_grad = (
        attn_out_grad
        + scale_one * weighted_one
        - hidden_in * scale_one**3 * jnp.mean(hidden_in * weighted_one, axis=-1, keepdims=True)
    )
    gain_sums = lax.psum(jnp.stack([gain_one_sum, gain_two_sum]), ("replica", "shard"))
    own_rows = width // lax.axis_size("shard")
    gain_own = lax.dynamic_slice_in_dim(
        gain_sums, lax.axis_index("shard") * own_rows, own_rows, axis=1
    )
    grads = weight_grads(
        normed_one, context, normed_two, out_grad, qkv_back, attn_low, gate_back, up_back, act
    )
    return (
        mixed,
        input_grad,
        gain_own[0],
        grads[0],
        grads[1],
        grads[2],
        grads[3],
        gain_own[1],
        grads[4],
        grads[5],
        grads[6],
    )


def solution(mesh):
    in_specs = (
        P(("replica", "shard"), None),
        P(("replica", "shard"), None),
        P("shard"),
        P("shard", None),
        P("shard", None),
        P("shard", None),
        P("shard", None),
        P("shard"),
        P("shard", None),
        P("shard", None),
        P("shard", None),
        P(("replica", "shard"), None),
    )
    out_specs = (
        P(("replica", "shard"), None),
        P(("replica", "shard"), None),
        P("shard"),
        P("shard", None),
        P("shard", None),
        P("shard", None),
        P("shard", None),
        P("shard"),
        P("shard", None),
        P("shard", None),
        P("shard", None),
    )
    return jax.shard_map(
        on_device, mesh=mesh, in_specs=in_specs, out_specs=out_specs, check_vma=False
    )
```

```python
import functools
import math

import jax
import jax.numpy as jnp
from jax import lax
from jax.experimental import pallas as pl
from jax.experimental.pallas import tpu as pltpu
from jax.sharding import PartitionSpec as P

HEADS = 15
KV_HEADS = 5
HEAD = 64


EPSILON = 1e-05
THETA = 100000.0


def layout(length_row, count):
    index_row = jnp.arange(count, dtype=jnp.int32)
    seq_ends = jnp.cumsum(length_row)
    seq_starts = seq_ends - length_row
    doc_index = jnp.sum((index_row[:, None] >= seq_ends[None, :]).astype(jnp.int32), axis=1)
    one_hot = doc_index[:, None] == jnp.arange(length_row.shape[0], dtype=jnp.int32)[None, :]
    first_slot = jnp.sum(jnp.where(one_hot, seq_starts[None, :], 0), axis=1)
    return (doc_index, index_row - first_slot)


def tables(positions, head_size):
    half_size = head_size // 2
    freq_index = jnp.arange(half_size, dtype=jnp.float32)
    inverse = THETA ** (-2.0 * freq_index / head_size)
    angles = positions.astype(jnp.float32)[..., None] * inverse
    return (jnp.cos(angles), jnp.sin(angles))


def rotate(values, cosine, sine):
    half_size = values.shape[-1] // 2
    first_half = values[..., :half_size]
    second_half = values[..., half_size:]
    cos_heads = cosine[:, None, :]
    sin_heads = sine[:, None, :]
    return jnp.concatenate(
        [
            first_half * cos_heads - second_half * sin_heads,
            second_half * cos_heads + first_half * sin_heads,
        ],
        axis=-1,
    )


def unrotate(grads, cosine, sine):
    half_size = grads.shape[-1] // 2
    first_half = grads[..., :half_size]
    second_half = grads[..., half_size:]
    cos_heads = cosine[:, None, :]
    sin_heads = sine[:, None, :]
    return jnp.concatenate(
        [
            first_half * cos_heads + second_half * sin_heads,
            second_half * cos_heads - first_half * sin_heads,
        ],
        axis=-1,
    )


def matmul(left, right):
    return jnp.dot(left, right, preferred_element_type=jnp.float32)


def matmul_right_t(left, right):
    return jnp.einsum("te,de->td", left, right, preferred_element_type=jnp.float32)


def matmul_left_t(left, right):
    return jnp.einsum("td,te->de", left, right, preferred_element_type=jnp.float32)


def masked_scores(query_rot, key_rot, allowed, score_scale):
    raw_scores = jnp.einsum(
        "tkhd,skd->khts", query_rot, key_rot, preferred_element_type=jnp.float32
    )
    return jnp.where(allowed[None, None], raw_scores * score_scale, -1e30)


UNIT = 16
MESH = pl.DeviceIdType.MESH


def piece_of(rows, n_replica, owner, act):
    units = rows // UNIT
    per_owner = -(-units // n_replica)
    full, rest = units // per_owner, units % per_owner
    start = pl.multiple_of(owner * (per_owner * UNIT), UNIT)
    if full == n_replica:
        act(start, per_owner * UNIT)
        return

    @pl.when(owner < full)
    def _():
        act(start, per_owner * UNIT)

    if rest:

        @pl.when(owner == full)
        def _():
            act(start, rest * UNIT)


def gather_kernel(n_replica, n_shard, n_arrays, *refs):
    shards, wides = refs[:n_arrays], refs[n_arrays : 2 * n_arrays]
    local_sem, line_sem, plane_sem, pair_sem, recv_sem = refs[2 * n_arrays :]
    me = lax.axis_index("replica")
    own = lax.axis_index("shard")
    n_chips = n_replica // 2
    core = lax.rem(me, 2)
    chip = me // 2
    partner = chip * 2 + (1 - core)
    line = [lax.rem(own + step, n_shard) for step in range(1, n_shard)]
    plane = [lax.rem(chip + step, n_chips) * 2 + core for step in range(1, n_chips)]

    barrier = pltpu.get_barrier_semaphore()
    for other in line:
        pl.semaphore_signal(
            barrier, inc=1, device_id={"replica": me, "shard": other}, device_id_type=MESH
        )
    for other in plane + [partner]:
        pl.semaphore_signal(
            barrier, inc=1, device_id={"replica": other, "shard": own}, device_id_type=MESH
        )
    pl.semaphore_wait(barrier, len(line) + len(plane) + 1)

    def line_copy(a, step, start, size):
        rows = pl.ds(start, size)
        return pltpu.make_async_remote_copy(
            src_ref=shards[a].at[rows],
            dst_ref=wides[a].at[own, rows],
            send_sem=line_sem.at[a, step],
            recv_sem=recv_sem.at[a, own, me],
            device_id={"replica": me, "shard": line[step]},
            device_id_type=MESH,
        )

    def spread(a, step, owner, target, send_sem, start, size):
        rows = pl.ds(start, size)
        block = wides[a].at[line[step], rows]
        return pltpu.make_async_remote_copy(
            src_ref=block,
            dst_ref=block,
            send_sem=send_sem,
            recv_sem=recv_sem.at[a, line[step], owner],
            device_id={"replica": target, "shard": own},
            device_id_type=MESH,
        )

    def wait_arrival(a, step, owner, start, size):
        spread(a, step, owner, partner, pair_sem.at[a, step, 0], start, size).wait_recv()

    def plane_copies(a, step, start, size):
        copies = [
            spread(a, step, me, other, plane_sem.at[a, step, i], start, size)
            for i, other in enumerate(plane)
        ]
        return copies + [spread(a, step, me, partner, pair_sem.at[a, step, 0], start, size)]

    def rows_of(a):
        return shards[a].shape[0]

    def send_plane(a):
        for step in range(n_shard - 1):

            def act(start, size, step=step):
                wait_arrival(a, step, me, start, size)
                for copy in plane_copies(a, step, start, size):
                    copy.start()

            piece_of(rows_of(a), n_replica, me, act)

    def send_pair(a):
        for step in range(n_shard - 1):
            for i, other in enumerate(plane):

                def act(start, size, step=step, i=i, other=other):
                    wait_arrival(a, step, other, start, size)
                    spread(
                        a, step, other, partner, pair_sem.at[a, step, i + 1], start, size
                    ).start()

                piece_of(rows_of(a), n_replica, other, act)

    def finish(a):
        for step in range(n_shard - 1):
            for i in range(n_chips):
                other = lax.rem(chip + i, n_chips) * 2 + 1 - core

                def arrived(start, size, step=step, other=other):
                    wait_arrival(a, step, other, start, size)

                piece_of(rows_of(a), n_replica, other, arrived)

            def sent(start, size, step=step):
                line_copy(a, step, start, size).wait_send()
                for copy in plane_copies(a, step, start, size):
                    copy.wait_send()

            piece_of(rows_of(a), n_replica, me, sent)
            for i, other in enumerate(plane):

                def passed(start, size, step=step, i=i, other=other):
                    spread(
                        a, step, other, partner, pair_sem.at[a, step, i + 1], start, size
                    ).wait_send()

                piece_of(rows_of(a), n_replica, other, passed)

    for a in range(n_arrays):

        def start_line(start, size, a=a):
            for step in range(n_shard - 1):
                line_copy(a, step, start, size).start()

        piece_of(rows_of(a), n_replica, me, start_line)
    locals_ = [
        pltpu.make_async_copy(shards[a], wides[a].at[own], local_sem.at[a])
        for a in range(n_arrays)
    ]
    for copy in locals_:
        copy.start()
    for a in range(n_arrays):
        send_plane(a)
        if a:
            send_pair(a - 1)
    send_pair(n_arrays - 1)
    for a in range(n_arrays):
        finish(a)
    for copy in locals_:
        copy.wait()


def gather_blocks(blocks):
    n_replica, n_shard = lax.axis_size("replica"), lax.axis_size("shard")
    n_arrays = len(blocks)
    n_chips = n_replica // 2
    dma = pltpu.SemaphoreType.DMA
    return pl.pallas_call(
        functools.partial(gather_kernel, n_replica, n_shard, n_arrays),
        out_shape=[
            jax.ShapeDtypeStruct((n_shard,) + block.shape, block.dtype) for block in blocks
        ],
        in_specs=[pl.BlockSpec(memory_space=pl.ANY)] * n_arrays,
        out_specs=[pl.BlockSpec(memory_space=pl.ANY)] * n_arrays,
        scratch_shapes=[
            dma((n_arrays,)),
            dma((n_arrays, n_shard - 1)),
            dma((n_arrays, n_shard - 1, n_chips - 1)),
            dma((n_arrays, n_shard - 1, n_chips)),
            dma((n_arrays, n_shard, n_replica)),
        ],
        compiler_params=pltpu.CompilerParams(collective_id=0, has_side_effects=True),
    )(*blocks)


def gather_weights(norm_one, norm_two, qkv_weight, output_weight, gate_weight, up_weight, down_weight):
    own_rows, width = output_weight.shape

    def padded(block, extra):
        rows = -(-(block.shape[0] + extra) // UNIT) * UNIT
        return jnp.pad(block, ((0, rows - block.shape[0]), (0, 0)))

    gains = jnp.pad(jnp.stack([norm_one, norm_two]), ((0, 0), (0, width - own_rows)))
    mixed_block = padded(jnp.concatenate([output_weight, gains]), 0)
    blocks = [mixed_block] + [
        padded(block, 0) for block in (qkv_weight, gate_weight, up_weight, down_weight)
    ]
    wide_mixed, *wides = gather_blocks(blocks)
    gain_one = wide_mixed[:, own_rows, :own_rows].reshape(-1)
    gain_two = wide_mixed[:, own_rows + 1, :own_rows].reshape(-1)

    def whole(wide, rows):
        return wide[:, :rows].reshape(-1, wide.shape[-1])

    return (
        gain_one,
        gain_two,
        whole(wides[0], own_rows),
        whole(wide_mixed, own_rows),
        whole(wides[1], own_rows),
        whole(wides[2], own_rows),
        whole(wides[3], down_weight.shape[0]),
    )


def weight_grads(
    normed_one, context, normed_two, out_grad, qkv_back, attn_low, gate_back, up_back, act
):
    n_replica = lax.axis_size("replica")
    n_shard = lax.axis_size("shard")
    count, width = normed_one.shape
    ff = act.shape[1]
    kv_width = KV_HEADS * HEAD

    def over_copies(rows):
        return lax.all_gather(rows, "replica", axis=0, tiled=True)

    def parts(columns):
        return columns.reshape(count, n_replica, -1)

    act_parts = act.reshape(count, n_shard, n_replica, -1).swapaxes(1, 2)
    columns = jnp.concatenate(
        [
            parts(gate_back),
            parts(up_back),
            act_parts.reshape(count, n_replica, -1),
            parts(qkv_back),
            parts(attn_low),
        ],
        axis=2,
    )
    columns = lax.all_to_all(columns, "replica", split_axis=1, concat_axis=0, tiled=True)
    columns = columns.reshape(n_replica * count, -1)
    ff_part = ff // n_replica
    qkv_part = qkv_back.shape[1] // n_replica
    out_part = width // n_replica
    cuts = [0, 2 * ff_part, 3 * ff_part, 3 * ff_part + qkv_part, columns.shape[1]]
    gate_up, act_cols, qkv_cols, out_cols = (
        columns[:, low:high] for low, high in zip(cuts[:-1], cuts[1:])
    )
    row_part = jnp.concatenate(
        [
            matmul_left_t(over_copies(normed_two), gate_up),
            matmul_left_t(over_copies(normed_one), qkv_cols),
            matmul_left_t(over_copies(context), out_cols),
        ],
        axis=1,
    ).astype(jnp.bfloat16)
    down_part = matmul_left_t(act_cols, over_copies(out_grad)).astype(jnp.bfloat16)
    own_rows = width // n_shard
    down_rows = ff_part // n_shard
    row_terms = lax.all_to_all(
        row_part.reshape(n_shard, own_rows, -1), "shard", split_axis=0, concat_axis=0, tiled=True
    )
    down_terms = lax.all_to_all(
        down_part.reshape(n_shard, down_rows, width),
        "shard",
        split_axis=0,
        concat_axis=0,
        tiled=True,
    )
    row_own = jnp.sum(row_terms.astype(jnp.float32), axis=0).astype(jnp.bfloat16)
    down_own = jnp.sum(down_terms.astype(jnp.float32), axis=0).astype(jnp.bfloat16)
    row_all = lax.all_gather(row_own, "replica", axis=0)
    down_all = lax.all_gather(down_own, "replica", axis=0, tiled=True)

    def whole(low, high):
        piece = row_all[:, :, low:high].swapaxes(0, 1).astype(jnp.float32)
        return piece.reshape(own_rows, -1)

    qkv_grad = whole(2 * ff_part, 2 * ff_part + qkv_part)
    return (
        qkv_grad[:, :width],
        qkv_grad[:, width : width + kv_width],
        qkv_grad[:, width + kv_width :],
        whole(2 * ff_part + qkv_part, 2 * ff_part + qkv_part + out_part),
        whole(0, ff_part),
        whole(ff_part, 2 * ff_part),
        down_all.astype(jnp.float32),
    )


def on_device(
    tokens,
    seq_lengths,
    norm_one,
    query_weight,
    key_weight,
    value_weight,
    output_weight,
    norm_two,
    gate_weight,
    up_weight,
    down_weight,
    out_grad,
):
    count, width = tokens.shape
    group_heads = HEADS // KV_HEADS
    score_scale = 1.0 / math.sqrt(HEAD)
    doc_index, positions = layout(seq_lengths[0], count)
    cosine, sine = tables(positions, HEAD)
    slots = jnp.arange(count, dtype=jnp.int32)
    allowed = (doc_index[:, None] == doc_index[None, :]) & (slots[:, None] >= slots[None, :])
    gain_one, gain_two, wide_qkv, wide_output, wide_gate, wide_up, wide_down = gather_weights(
        norm_one,
        norm_two,
        jnp.concatenate([query_weight, key_weight, value_weight], axis=1),
        output_weight,
        gate_weight,
        up_weight,
        down_weight,
    )
    hidden_in = tokens.astype(jnp.float32)
    scale_one = lax.rsqrt(jnp.mean(hidden_in * hidden_in, axis=-1, keepdims=True) + EPSILON)
    normed_one = (hidden_in * scale_one * gain_one.astype(jnp.float32)).astype(jnp.bfloat16)
    qkv_pre = matmul(normed_one, wide_qkv)
    kv_width = KV_HEADS * HEAD
    queries_pre = qkv_pre[:, :width].reshape(count, HEADS, HEAD)
    query_rot = (
        rotate(queries_pre, cosine, sine)
        .astype(jnp.bfloat16)
        .reshape(count, KV_HEADS, group_heads, HEAD)
    )
    keys_pre = qkv_pre[:, width : width + kv_width].reshape(count, KV_HEADS, HEAD)
    key_rot = rotate(keys_pre, cosine, sine).astype(jnp.bfloat16)
    value_rot = qkv_pre[:, width + kv_width :].astype(jnp.bfloat16).reshape(count, KV_HEADS, HEAD)
    scores = masked_scores(query_rot, key_rot, allowed, score_scale)
    log_total = jax.nn.logsumexp(scores, axis=-1, keepdims=True)
    probs_low = jnp.exp(scores - log_total).astype(jnp.bfloat16)
    context = jnp.einsum("khts,skd->tkhd", probs_low, value_rot, preferred_element_type=jnp.float32)
    context = context.reshape(count, width).astype(jnp.bfloat16)
    after_attn = hidden_in + matmul(context, wide_output)
    scale_two = lax.rsqrt(jnp.mean(after_attn * after_attn, axis=-1, keepdims=True) + EPSILON)
    normed_two = (after_attn * scale_two * gain_two.astype(jnp.float32)).astype(jnp.bfloat16)
    gate_pre = matmul(normed_two, wide_gate)
    up_pre = matmul(normed_two, wide_up)
    sigmoid_gate = jax.nn.sigmoid(gate_pre)
    silu_gate = gate_pre * sigmoid_gate
    act = (silu_gate * up_pre).astype(jnp.bfloat16)
    mixed = (after_attn + matmul(act, wide_down)).astype(jnp.bfloat16)
    cotangent = out_grad.astype(jnp.float32)
    act_grad = matmul_right_t(out_grad, wide_down)
    gate_back = (act_grad * up_pre * sigmoid_gate * (1.0 + gate_pre * (1.0 - sigmoid_gate))).astype(
        jnp.bfloat16
    )
    up_back = (act_grad * silu_gate).astype(jnp.bfloat16)
    normed_two_grad = matmul_right_t(gate_back, wide_gate) + matmul_right_t(up_back, wide_up)
    gain_two_sum = jnp.sum(normed_two_grad * after_attn * scale_two, axis=0)
    weighted_two = normed_two_grad * gain_two.astype(jnp.float32)
    attn_out_grad = (
        cotangent
        + scale_two * weighted_two
        - after_attn * scale_two**3 * jnp.mean(after_attn * weighted_two, axis=-1, keepdims=True)
    )
    attn_low = attn_out_grad.astype(jnp.bfloat16)
    context_grad = (
        matmul_right_t(attn_low, wide_output)
        .astype(jnp.bfloat16)
        .reshape(count, KV_HEADS, group_heads, HEAD)
    )
    scores = masked_scores(query_rot, key_rot, allowed, score_scale)
    probs = jnp.exp(scores - log_total)
    probs_low = probs.astype(jnp.bfloat16)
    value_back = jnp.einsum(
        "khts,tkhd->skd", probs_low, context_grad, preferred_element_type=jnp.float32
    )
    value_back = value_back.reshape(count, KV_HEADS * HEAD).astype(jnp.bfloat16)
    probs_grad = jnp.einsum(
        "tkhd,skd->khts", context_grad, value_rot, preferred_element_type=jnp.float32
    )
    row_inner = jnp.sum(probs * probs_grad, axis=-1, keepdims=True)
    score_back = (probs * (probs_grad - row_inner) * score_scale).astype(jnp.bfloat16)
    query_rot_grad = jnp.einsum(
        "khts,skd->tkhd", score_back, key_rot, preferred_element_type=jnp.float32
    )
    key_rot_grad = jnp.einsum(
        "khts,tkhd->skd", score_back, query_rot, preferred_element_type=jnp.float32
    )
    query_back = (
        unrotate(query_rot_grad.reshape(count, HEADS, HEAD), cosine, sine)
        .reshape(count, width)
        .astype(jnp.bfloat16)
    )
    key_back = (
        unrotate(key_rot_grad, cosine, sine).reshape(count, KV_HEADS * HEAD).astype(jnp.bfloat16)
    )
    qkv_back = jnp.concatenate([query_back, key_back, value_back], axis=1)
    normed_one_grad = matmul_right_t(qkv_back, wide_qkv)
    gain_one_sum = jnp.sum(normed_one_grad * hidden_in * scale_one, axis=0)
    weighted_one = normed_one_grad * gain_one.astype(jnp.float32)
    input_grad = (
        attn_out_grad
        + scale_one * weighted_one
        - hidden_in * scale_one**3 * jnp.mean(hidden_in * weighted_one, axis=-1, keepdims=True)
    )
    gain_sums = lax.psum(jnp.stack([gain_one_sum, gain_two_sum]), ("replica", "shard"))
    own_rows = width // lax.axis_size("shard")
    gain_own = lax.dynamic_slice_in_dim(
        gain_sums, lax.axis_index("shard") * own_rows, own_rows, axis=1
    )
    grads = weight_grads(
        normed_one, context, normed_two, out_grad, qkv_back, attn_low, gate_back, up_back, act
    )
    return (
        mixed,
        input_grad,
        gain_own[0],
        grads[0],
        grads[1],
        grads[2],
        grads[3],
        gain_own[1],
        grads[4],
        grads[5],
        grads[6],
    )


def solution(mesh):
    in_specs = (
        P(("replica", "shard"), None),
        P(("replica", "shard"), None),
        P("shard"),
        P("shard", None),
        P("shard", None),
        P("shard", None),
        P("shard", None),
        P("shard"),
        P("shard", None),
        P("shard", None),
        P("shard", None),
        P(("replica", "shard"), None),
    )
    out_specs = (
        P(("replica", "shard"), None),
        P(("replica", "shard"), None),
        P("shard"),
        P("shard", None),
        P("shard", None),
        P("shard", None),
        P("shard", None),
        P("shard"),
        P("shard", None),
        P("shard", None),
        P("shard", None),
    )
    return jax.shard_map(
        on_device, mesh=mesh, in_specs=in_specs, out_specs=out_specs, check_vma=False
    )
```

```python
import functools
import math

import jax
import jax.numpy as jnp
from jax import lax
from jax.experimental import pallas as pl
from jax.experimental.pallas import tpu as pltpu
from jax.sharding import PartitionSpec as P

HEADS = 15
KV_HEADS = 5
HEAD = 64


EPSILON = 1e-05
THETA = 100000.0


def layout(length_row, count):
    index_row = jnp.arange(count, dtype=jnp.int32)
    seq_ends = jnp.cumsum(length_row)
    seq_starts = seq_ends - length_row
    doc_index = jnp.sum((index_row[:, None] >= seq_ends[None, :]).astype(jnp.int32), axis=1)
    one_hot = doc_index[:, None] == jnp.arange(length_row.shape[0], dtype=jnp.int32)[None, :]
    first_slot = jnp.sum(jnp.where(one_hot, seq_starts[None, :], 0), axis=1)
    return (doc_index, index_row - first_slot)


def tables(positions, head_size):
    half_size = head_size // 2
    freq_index = jnp.arange(half_size, dtype=jnp.float32)
    inverse = THETA ** (-2.0 * freq_index / head_size)
    angles = positions.astype(jnp.float32)[..., None] * inverse
    return (jnp.cos(angles), jnp.sin(angles))


def rotate(values, cosine, sine):
    half_size = values.shape[-1] // 2
    first_half = values[..., :half_size]
    second_half = values[..., half_size:]
    cos_heads = cosine[:, None, :]
    sin_heads = sine[:, None, :]
    return jnp.concatenate(
        [
            first_half * cos_heads - second_half * sin_heads,
            second_half * cos_heads + first_half * sin_heads,
        ],
        axis=-1,
    )


def unrotate(grads, cosine, sine):
    half_size = grads.shape[-1] // 2
    first_half = grads[..., :half_size]
    second_half = grads[..., half_size:]
    cos_heads = cosine[:, None, :]
    sin_heads = sine[:, None, :]
    return jnp.concatenate(
        [
            first_half * cos_heads + second_half * sin_heads,
            second_half * cos_heads - first_half * sin_heads,
        ],
        axis=-1,
    )


def matmul(left, right):
    return jnp.dot(left, right, preferred_element_type=jnp.float32)


def matmul_right_t(left, right):
    return jnp.einsum("te,de->td", left, right, preferred_element_type=jnp.float32)


def matmul_left_t(left, right):
    return jnp.einsum("td,te->de", left, right, preferred_element_type=jnp.float32)


def masked_scores(query_rot, key_rot, allowed, score_scale):
    raw_scores = jnp.einsum(
        "tkhd,skd->khts", query_rot, key_rot, preferred_element_type=jnp.float32
    )
    return jnp.where(allowed[None, None], raw_scores * score_scale, -1e30)


UNIT = 16
MESH = pl.DeviceIdType.MESH


def piece_of(rows, n_replica, owner, act):
    units = rows // UNIT
    per_owner = -(-units // n_replica)
    full, rest = units // per_owner, units % per_owner
    start = pl.multiple_of(owner * (per_owner * UNIT), UNIT)
    if full == n_replica:
        act(start, per_owner * UNIT)
        return

    @pl.when(owner < full)
    def _():
        act(start, per_owner * UNIT)

    if rest:

        @pl.when(owner == full)
        def _():
            act(start, rest * UNIT)


def gather_kernel(n_replica, n_shard, n_arrays, *refs):
    shards, wides = refs[:n_arrays], refs[n_arrays : 2 * n_arrays]
    local_sem, line_sem, plane_sem, pair_sem, recv_sem = refs[2 * n_arrays :]
    me = lax.axis_index("replica")
    own = lax.axis_index("shard")
    n_chips = n_replica // 2
    core = lax.rem(me, 2)
    chip = me // 2
    partner = chip * 2 + (1 - core)
    line = [lax.rem(own + step, n_shard) for step in range(1, n_shard)]
    plane = [lax.rem(chip + step, n_chips) * 2 + core for step in range(1, n_chips)]

    barrier = pltpu.get_barrier_semaphore()
    for other in line:
        pl.semaphore_signal(
            barrier, inc=1, device_id={"replica": me, "shard": other}, device_id_type=MESH
        )
    for other in plane + [partner]:
        pl.semaphore_signal(
            barrier, inc=1, device_id={"replica": other, "shard": own}, device_id_type=MESH
        )
    pl.semaphore_wait(barrier, len(line) + len(plane) + 1)

    def line_copy(a, step, start, size):
        rows = pl.ds(start, size)
        return pltpu.make_async_remote_copy(
            src_ref=shards[a].at[rows],
            dst_ref=wides[a].at[own, rows],
            send_sem=line_sem.at[a, step],
            recv_sem=recv_sem.at[a, own, me],
            device_id={"replica": me, "shard": line[step]},
            device_id_type=MESH,
        )

    def spread(a, step, owner, target, send_sem, start, size):
        rows = pl.ds(start, size)
        block = wides[a].at[line[step], rows]
        return pltpu.make_async_remote_copy(
            src_ref=block,
            dst_ref=block,
            send_sem=send_sem,
            recv_sem=recv_sem.at[a, line[step], owner],
            device_id={"replica": target, "shard": own},
            device_id_type=MESH,
        )

    def wait_arrival(a, step, owner, start, size):
        spread(a, step, owner, partner, pair_sem.at[a, step, 0], start, size).wait_recv()

    def plane_copies(a, step, start, size):
        copies = [
            spread(a, step, me, other, plane_sem.at[a, step, i], start, size)
            for i, other in enumerate(plane)
        ]
        return copies + [spread(a, step, me, partner, pair_sem.at[a, step, 0], start, size)]

    def rows_of(a):
        return shards[a].shape[0]

    def send_plane(a):
        for step in range(n_shard - 1):

            def act(start, size, step=step):
                wait_arrival(a, step, me, start, size)
                for copy in plane_copies(a, step, start, size):
                    copy.start()

            piece_of(rows_of(a), n_replica, me, act)

    def send_pair(a):
        for step in range(n_shard - 1):
            for i, other in enumerate(plane):

                def act(start, size, step=step, i=i, other=other):
                    wait_arrival(a, step, other, start, size)
                    spread(
                        a, step, other, partner, pair_sem.at[a, step, i + 1], start, size
                    ).start()

                piece_of(rows_of(a), n_replica, other, act)

    def finish(a):
        for step in range(n_shard - 1):
            for i in range(n_chips):
                other = lax.rem(chip + i, n_chips) * 2 + 1 - core

                def arrived(start, size, step=step, other=other):
                    wait_arrival(a, step, other, start, size)

                piece_of(rows_of(a), n_replica, other, arrived)

            def sent(start, size, step=step):
                line_copy(a, step, start, size).wait_send()
                for copy in plane_copies(a, step, start, size):
                    copy.wait_send()

            piece_of(rows_of(a), n_replica, me, sent)
            for i, other in enumerate(plane):

                def passed(start, size, step=step, i=i, other=other):
                    spread(
                        a, step, other, partner, pair_sem.at[a, step, i + 1], start, size
                    ).wait_send()

                piece_of(rows_of(a), n_replica, other, passed)

    def send_line(a):
        def start_line(start, size):
            for step in range(n_shard - 1):
                line_copy(a, step, start, size).start()

        piece_of(rows_of(a), n_replica, me, start_line)

    for a in range(min(2, n_arrays)):
        send_line(a)
    locals_ = [
        pltpu.make_async_copy(shards[a], wides[a].at[own], local_sem.at[a])
        for a in range(n_arrays)
    ]
    for copy in locals_:
        copy.start()
    for a in range(n_arrays):
        send_plane(a)
        if a + 2 < n_arrays:
            send_line(a + 2)
        if a:
            send_pair(a - 1)
    send_pair(n_arrays - 1)
    for a in range(n_arrays):
        finish(a)
    for copy in locals_:
        copy.wait()


def gather_blocks(blocks):
    n_replica, n_shard = lax.axis_size("replica"), lax.axis_size("shard")
    n_arrays = len(blocks)
    n_chips = n_replica // 2
    dma = pltpu.SemaphoreType.DMA
    return pl.pallas_call(
        functools.partial(gather_kernel, n_replica, n_shard, n_arrays),
        out_shape=[
            jax.ShapeDtypeStruct((n_shard,) + block.shape, block.dtype) for block in blocks
        ],
        in_specs=[pl.BlockSpec(memory_space=pl.ANY)] * n_arrays,
        out_specs=[pl.BlockSpec(memory_space=pl.ANY)] * n_arrays,
        scratch_shapes=[
            dma((n_arrays,)),
            dma((n_arrays, n_shard - 1)),
            dma((n_arrays, n_shard - 1, n_chips - 1)),
            dma((n_arrays, n_shard - 1, n_chips)),
            dma((n_arrays, n_shard, n_replica)),
        ],
        compiler_params=pltpu.CompilerParams(collective_id=0, has_side_effects=True),
    )(*blocks)


def gather_weights(norm_one, norm_two, qkv_weight, output_weight, gate_weight, up_weight, down_weight):
    own_rows, width = output_weight.shape

    def padded(block, extra):
        rows = -(-(block.shape[0] + extra) // UNIT) * UNIT
        return jnp.pad(block, ((0, rows - block.shape[0]), (0, 0)))

    gains = jnp.pad(jnp.stack([norm_one, norm_two]), ((0, 0), (0, width - own_rows)))
    mixed_block = padded(jnp.concatenate([output_weight, gains]), 0)
    blocks = [mixed_block] + [
        padded(block, 0) for block in (qkv_weight, gate_weight, up_weight, down_weight)
    ]
    wide_mixed, *wides = gather_blocks(blocks)
    gain_one = wide_mixed[:, own_rows, :own_rows].reshape(-1)
    gain_two = wide_mixed[:, own_rows + 1, :own_rows].reshape(-1)

    def whole(wide, rows):
        return wide[:, :rows].reshape(-1, wide.shape[-1])

    return (
        gain_one,
        gain_two,
        whole(wides[0], own_rows),
        whole(wide_mixed, own_rows),
        whole(wides[1], own_rows),
        whole(wides[2], own_rows),
        whole(wides[3], down_weight.shape[0]),
    )


def over_copies(rows):
    return lax.all_gather(rows, "replica", axis=0, tiled=True)


def exchange_columns(members):
    n_replica = lax.axis_size("replica")
    count = members[0].shape[0]
    columns = jnp.concatenate(
        [member.reshape(count, n_replica, -1) for member in members], axis=2
    )
    columns = lax.all_to_all(columns, "replica", split_axis=1, concat_axis=0, tiled=True)
    return columns.reshape(n_replica * count, -1)


def sum_over_shard(part, n_rows):
    n_shard = lax.axis_size("shard")
    terms = lax.all_to_all(
        part.astype(jnp.bfloat16).reshape(n_shard, n_rows, -1),
        "shard",
        split_axis=0,
        concat_axis=0,
        tiled=True,
    )
    return jnp.sum(terms.astype(jnp.float32), axis=0).astype(jnp.bfloat16)


def feed_grads(normed_two, out_grad, gate_back, up_back, act):
    n_replica = lax.axis_size("replica")
    n_shard = lax.axis_size("shard")
    count, width = normed_two.shape
    ff_part = act.shape[1] // n_replica
    act_parts = act.reshape(count, n_shard, n_replica, -1).swapaxes(1, 2)
    columns = exchange_columns([gate_back, up_back, act_parts])
    row_part = matmul_left_t(over_copies(normed_two), columns[:, : 2 * ff_part])
    down_part = matmul_left_t(columns[:, 2 * ff_part :], over_copies(out_grad))
    row_all = lax.all_gather(sum_over_shard(row_part, width // n_shard), "replica", axis=0)
    down_all = over_copies(sum_over_shard(down_part, ff_part // n_shard))
    return row_all, down_all.astype(jnp.float32)


def attention_grads(normed_one, context, qkv_back, attn_low):
    n_replica = lax.axis_size("replica")
    n_shard = lax.axis_size("shard")
    width = normed_one.shape[1]
    qkv_part = qkv_back.shape[1] // n_replica
    columns = exchange_columns([qkv_back, attn_low])
    row_part = jnp.concatenate(
        [
            matmul_left_t(over_copies(normed_one), columns[:, :qkv_part]),
            matmul_left_t(over_copies(context), columns[:, qkv_part:]),
        ],
        axis=1,
    )
    return lax.all_gather(sum_over_shard(row_part, width // n_shard), "replica", axis=0)


def unpack_kernel(widths, feed_ref, attn_ref, *out_refs):
    n_replica = feed_ref.shape[0]
    query_ref, key_ref, value_ref, output_ref, gate_ref, up_ref = out_refs
    feed = [feed_ref[part].astype(jnp.float32) for part in range(n_replica)]
    attn = [attn_ref[part].astype(jnp.float32) for part in range(n_replica)]
    ff_part = feed[0].shape[1] // 2
    qkv_part = sum(widths) // n_replica
    gate_ref[...] = jnp.concatenate([piece[:, :ff_part] for piece in feed], axis=1)
    up_ref[...] = jnp.concatenate([piece[:, ff_part:] for piece in feed], axis=1)
    output_ref[...] = jnp.concatenate([piece[:, qkv_part:] for piece in attn], axis=1)
    qkv = jnp.concatenate([piece[:, :qkv_part] for piece in attn], axis=1)
    low = 0
    for ref, width in zip((query_ref, key_ref, value_ref), widths):
        ref[...] = qkv[:, low : low + width]
        low += width


def unpack(feed_all, attn_all, width, kv_width):
    n_replica, rows, feed_cols = feed_all.shape
    attn_cols = attn_all.shape[2]
    step = 48 if rows % 48 == 0 else rows
    ff = feed_cols * n_replica // 2
    out_widths = (width, kv_width, kv_width, width, ff, ff)
    return pl.pallas_call(
        functools.partial(unpack_kernel, out_widths[:3]),
        grid=(rows // step,),
        out_shape=[jax.ShapeDtypeStruct((rows, cols), jnp.float32) for cols in out_widths],
        in_specs=[
            pl.BlockSpec((n_replica, step, feed_cols), lambda i: (0, i, 0)),
            pl.BlockSpec((n_replica, step, attn_cols), lambda i: (0, i, 0)),
        ],
        out_specs=[pl.BlockSpec((step, cols), lambda i: (i, 0)) for cols in out_widths],
        compiler_params=pltpu.CompilerParams(vmem_limit_bytes=32 * 1024 * 1024),
    )(feed_all, attn_all)


def on_device(
    tokens,
    seq_lengths,
    norm_one,
    query_weight,
    key_weight,
    value_weight,
    output_weight,
    norm_two,
    gate_weight,
    up_weight,
    down_weight,
    out_grad,
):
    count, width = tokens.shape
    group_heads = HEADS // KV_HEADS
    score_scale = 1.0 / math.sqrt(HEAD)
    doc_index, positions = layout(seq_lengths[0], count)
    cosine, sine = tables(positions, HEAD)
    slots = jnp.arange(count, dtype=jnp.int32)
    allowed = (doc_index[:, None] == doc_index[None, :]) & (slots[:, None] >= slots[None, :])
    gain_one, gain_two, wide_qkv, wide_output, wide_gate, wide_up, wide_down = gather_weights(
        norm_one,
        norm_two,
        jnp.concatenate([query_weight, key_weight, value_weight], axis=1),
        output_weight,
        gate_weight,
        up_weight,
        down_weight,
    )
    hidden_in = tokens.astype(jnp.float32)
    scale_one = lax.rsqrt(jnp.mean(hidden_in * hidden_in, axis=-1, keepdims=True) + EPSILON)
    normed_one = (hidden_in * scale_one * gain_one.astype(jnp.float32)).astype(jnp.bfloat16)
    qkv_pre = matmul(normed_one, wide_qkv)
    kv_width = KV_HEADS * HEAD
    queries_pre = qkv_pre[:, :width].reshape(count, HEADS, HEAD)
    query_rot = (
        rotate(queries_pre, cosine, sine)
        .astype(jnp.bfloat16)
        .reshape(count, KV_HEADS, group_heads, HEAD)
    )
    keys_pre = qkv_pre[:, width : width + kv_width].reshape(count, KV_HEADS, HEAD)
    key_rot = rotate(keys_pre, cosine, sine).astype(jnp.bfloat16)
    value_rot = qkv_pre[:, width + kv_width :].astype(jnp.bfloat16).reshape(count, KV_HEADS, HEAD)
    scores = masked_scores(query_rot, key_rot, allowed, score_scale)
    log_total = jax.nn.logsumexp(scores, axis=-1, keepdims=True)
    probs_low = jnp.exp(scores - log_total).astype(jnp.bfloat16)
    context = jnp.einsum("khts,skd->tkhd", probs_low, value_rot, preferred_element_type=jnp.float32)
    context = context.reshape(count, width).astype(jnp.bfloat16)
    after_attn = hidden_in + matmul(context, wide_output)
    scale_two = lax.rsqrt(jnp.mean(after_attn * after_attn, axis=-1, keepdims=True) + EPSILON)
    normed_two = (after_attn * scale_two * gain_two.astype(jnp.float32)).astype(jnp.bfloat16)
    gate_pre = matmul(normed_two, wide_gate)
    up_pre = matmul(normed_two, wide_up)
    sigmoid_gate = jax.nn.sigmoid(gate_pre)
    silu_gate = gate_pre * sigmoid_gate
    act = (silu_gate * up_pre).astype(jnp.bfloat16)
    mixed = (after_attn + matmul(act, wide_down)).astype(jnp.bfloat16)
    cotangent = out_grad.astype(jnp.float32)
    act_grad = matmul_right_t(out_grad, wide_down)
    gate_back = (act_grad * up_pre * sigmoid_gate * (1.0 + gate_pre * (1.0 - sigmoid_gate))).astype(
        jnp.bfloat16
    )
    up_back = (act_grad * silu_gate).astype(jnp.bfloat16)
    normed_two_grad = matmul_right_t(gate_back, wide_gate) + matmul_right_t(up_back, wide_up)
    gain_two_sum = jnp.sum(normed_two_grad * after_attn * scale_two, axis=0)
    weighted_two = normed_two_grad * gain_two.astype(jnp.float32)
    attn_out_grad = (
        cotangent
        + scale_two * weighted_two
        - after_attn * scale_two**3 * jnp.mean(after_attn * weighted_two, axis=-1, keepdims=True)
    )
    feed_all, down_grad = feed_grads(normed_two, out_grad, gate_back, up_back, act)
    attn_low = attn_out_grad.astype(jnp.bfloat16)
    context_grad = (
        matmul_right_t(attn_low, wide_output)
        .astype(jnp.bfloat16)
        .reshape(count, KV_HEADS, group_heads, HEAD)
    )
    scores = masked_scores(query_rot, key_rot, allowed, score_scale)
    probs = jnp.exp(scores - log_total)
    probs_low = probs.astype(jnp.bfloat16)
    value_back = jnp.einsum(
        "khts,tkhd->skd", probs_low, context_grad, preferred_element_type=jnp.float32
    )
    value_back = value_back.reshape(count, KV_HEADS * HEAD).astype(jnp.bfloat16)
    probs_grad = jnp.einsum(
        "tkhd,skd->khts", context_grad, value_rot, preferred_element_type=jnp.float32
    )
    row_inner = jnp.sum(probs * probs_grad, axis=-1, keepdims=True)
    score_back = (probs * (probs_grad - row_inner) * score_scale).astype(jnp.bfloat16)
    query_rot_grad = jnp.einsum(
        "khts,skd->tkhd", score_back, key_rot, preferred_element_type=jnp.float32
    )
    key_rot_grad = jnp.einsum(
        "khts,tkhd->skd", score_back, query_rot, preferred_element_type=jnp.float32
    )
    query_back = (
        unrotate(query_rot_grad.reshape(count, HEADS, HEAD), cosine, sine)
        .reshape(count, width)
        .astype(jnp.bfloat16)
    )
    key_back = (
        unrotate(key_rot_grad, cosine, sine).reshape(count, KV_HEADS * HEAD).astype(jnp.bfloat16)
    )
    qkv_back = jnp.concatenate([query_back, key_back, value_back], axis=1)
    normed_one_grad = matmul_right_t(qkv_back, wide_qkv)
    gain_one_sum = jnp.sum(normed_one_grad * hidden_in * scale_one, axis=0)
    weighted_one = normed_one_grad * gain_one.astype(jnp.float32)
    input_grad = (
        attn_out_grad
        + scale_one * weighted_one
        - hidden_in * scale_one**3 * jnp.mean(hidden_in * weighted_one, axis=-1, keepdims=True)
    )
    gain_sums = lax.psum(jnp.stack([gain_one_sum, gain_two_sum]), ("replica", "shard"))
    own_rows = width // lax.axis_size("shard")
    gain_own = lax.dynamic_slice_in_dim(
        gain_sums, lax.axis_index("shard") * own_rows, own_rows, axis=1
    )
    attn_all = attention_grads(normed_one, context, qkv_back, attn_low)
    grads = unpack(feed_all, attn_all, width, kv_width)
    return (
        mixed,
        input_grad,
        gain_own[0],
        grads[0],
        grads[1],
        grads[2],
        grads[3],
        gain_own[1],
        grads[4],
        grads[5],
        down_grad,
    )


def solution(mesh):
    in_specs = (
        P(("replica", "shard"), None),
        P(("replica", "shard"), None),
        P("shard"),
        P("shard", None),
        P("shard", None),
        P("shard", None),
        P("shard", None),
        P("shard"),
        P("shard", None),
        P("shard", None),
        P("shard", None),
        P(("replica", "shard"), None),
    )
    out_specs = (
        P(("replica", "shard"), None),
        P(("replica", "shard"), None),
        P("shard"),
        P("shard", None),
        P("shard", None),
        P("shard", None),
        P("shard", None),
        P("shard"),
        P("shard", None),
        P("shard", None),
        P("shard", None),
    )
    return jax.shard_map(
        on_device, mesh=mesh, in_specs=in_specs, out_specs=out_specs, check_vma=False
    )
```

```python
import functools
import math

import jax
import jax.numpy as jnp
from jax import lax
from jax.experimental import pallas as pl
from jax.experimental.pallas import tpu as pltpu
from jax.sharding import PartitionSpec as P

HEADS = 15
KV_HEADS = 5
HEAD = 64


EPSILON = 1e-05
THETA = 100000.0


def layout(length_row, count):
    index_row = jnp.arange(count, dtype=jnp.int32)
    seq_ends = jnp.cumsum(length_row)
    seq_starts = seq_ends - length_row
    doc_index = jnp.sum((index_row[:, None] >= seq_ends[None, :]).astype(jnp.int32), axis=1)
    one_hot = doc_index[:, None] == jnp.arange(length_row.shape[0], dtype=jnp.int32)[None, :]
    first_slot = jnp.sum(jnp.where(one_hot, seq_starts[None, :], 0), axis=1)
    return (doc_index, index_row - first_slot)


def tables(positions, head_size):
    half_size = head_size // 2
    freq_index = jnp.arange(half_size, dtype=jnp.float32)
    inverse = THETA ** (-2.0 * freq_index / head_size)
    angles = positions.astype(jnp.float32)[..., None] * inverse
    return (jnp.cos(angles), jnp.sin(angles))


def rotate(values, cosine, sine):
    half_size = values.shape[-1] // 2
    first_half = values[..., :half_size]
    second_half = values[..., half_size:]
    cos_heads = cosine[:, None, :]
    sin_heads = sine[:, None, :]
    return jnp.concatenate(
        [
            first_half * cos_heads - second_half * sin_heads,
            second_half * cos_heads + first_half * sin_heads,
        ],
        axis=-1,
    )


def unrotate(grads, cosine, sine):
    half_size = grads.shape[-1] // 2
    first_half = grads[..., :half_size]
    second_half = grads[..., half_size:]
    cos_heads = cosine[:, None, :]
    sin_heads = sine[:, None, :]
    return jnp.concatenate(
        [
            first_half * cos_heads + second_half * sin_heads,
            second_half * cos_heads - first_half * sin_heads,
        ],
        axis=-1,
    )


def matmul(left, right):
    return jnp.dot(left, right, preferred_element_type=jnp.float32)


def matmul_right_t(left, right):
    return jnp.einsum("te,de->td", left, right, preferred_element_type=jnp.float32)


def matmul_left_t(left, right):
    return jnp.einsum("td,te->de", left, right, preferred_element_type=jnp.float32)


def masked_scores(query_rot, key_rot, allowed, score_scale):
    raw_scores = jnp.einsum(
        "tkhd,skd->khts", query_rot, key_rot, preferred_element_type=jnp.float32
    )
    return jnp.where(allowed[None, None], raw_scores * score_scale, -1e30)


UNIT = 16
MESH = pl.DeviceIdType.MESH


def piece_of(rows, n_replica, owner, act):
    units = rows // UNIT
    per_owner = -(-units // n_replica)
    full, rest = units // per_owner, units % per_owner
    start = pl.multiple_of(owner * (per_owner * UNIT), UNIT)
    if full == n_replica:
        act(start, per_owner * UNIT)
        return

    @pl.when(owner < full)
    def _():
        act(start, per_owner * UNIT)

    if rest:

        @pl.when(owner == full)
        def _():
            act(start, rest * UNIT)


def gather_kernel(n_replica, n_shard, n_arrays, *refs):
    shards, wides = refs[:n_arrays], refs[n_arrays : 2 * n_arrays]
    local_sem, line_sem, plane_sem, pair_sem, recv_sem = refs[2 * n_arrays :]
    me = lax.axis_index("replica")
    own = lax.axis_index("shard")
    n_chips = n_replica // 2
    core = lax.rem(me, 2)
    chip = me // 2
    partner = chip * 2 + (1 - core)
    line = [lax.rem(own + step, n_shard) for step in range(1, n_shard)]
    plane = [lax.rem(chip + step, n_chips) * 2 + core for step in range(1, n_chips)]

    barrier = pltpu.get_barrier_semaphore()
    for other in line:
        pl.semaphore_signal(
            barrier, inc=1, device_id={"replica": me, "shard": other}, device_id_type=MESH
        )
    for other in plane + [partner]:
        pl.semaphore_signal(
            barrier, inc=1, device_id={"replica": other, "shard": own}, device_id_type=MESH
        )
    pl.semaphore_wait(barrier, len(line) + len(plane) + 1)

    def line_copy(a, step, start, size):
        rows = pl.ds(start, size)
        return pltpu.make_async_remote_copy(
            src_ref=shards[a].at[rows],
            dst_ref=wides[a].at[own, rows],
            send_sem=line_sem.at[a, step],
            recv_sem=recv_sem.at[a, own, me],
            device_id={"replica": me, "shard": line[step]},
            device_id_type=MESH,
        )

    def spread(a, step, owner, target, send_sem, start, size):
        rows = pl.ds(start, size)
        block = wides[a].at[line[step], rows]
        return pltpu.make_async_remote_copy(
            src_ref=block,
            dst_ref=block,
            send_sem=send_sem,
            recv_sem=recv_sem.at[a, line[step], owner],
            device_id={"replica": target, "shard": own},
            device_id_type=MESH,
        )

    def wait_arrival(a, step, owner, start, size):
        spread(a, step, owner, partner, pair_sem.at[a, step, 0], start, size).wait_recv()

    def plane_copies(a, step, start, size):
        copies = [
            spread(a, step, me, other, plane_sem.at[a, step, i], start, size)
            for i, other in enumerate(plane)
        ]
        return copies + [spread(a, step, me, partner, pair_sem.at[a, step, 0], start, size)]

    def rows_of(a):
        return shards[a].shape[0]

    def send_plane(a):
        for step in range(n_shard - 1):

            def act(start, size, step=step):
                wait_arrival(a, step, me, start, size)
                for copy in plane_copies(a, step, start, size):
                    copy.start()

            piece_of(rows_of(a), n_replica, me, act)

    def send_pair(a):
        for step in range(n_shard - 1):
            for i, other in enumerate(plane):

                def act(start, size, step=step, i=i, other=other):
                    wait_arrival(a, step, other, start, size)
                    spread(
                        a, step, other, partner, pair_sem.at[a, step, i + 1], start, size
                    ).start()

                piece_of(rows_of(a), n_replica, other, act)

    def finish(a):
        for step in range(n_shard - 1):
            for i in range(n_chips):
                other = lax.rem(chip + i, n_chips) * 2 + 1 - core

                def arrived(start, size, step=step, other=other):
                    wait_arrival(a, step, other, start, size)

                piece_of(rows_of(a), n_replica, other, arrived)

            def sent(start, size, step=step):
                line_copy(a, step, start, size).wait_send()
                for copy in plane_copies(a, step, start, size):
                    copy.wait_send()

            piece_of(rows_of(a), n_replica, me, sent)
            for i, other in enumerate(plane):

                def passed(start, size, step=step, i=i, other=other):
                    spread(
                        a, step, other, partner, pair_sem.at[a, step, i + 1], start, size
                    ).wait_send()

                piece_of(rows_of(a), n_replica, other, passed)

    def send_line(a):
        def start_line(start, size):
            for step in range(n_shard - 1):
                line_copy(a, step, start, size).start()

        piece_of(rows_of(a), n_replica, me, start_line)

    for a in range(min(2, n_arrays)):
        send_line(a)
    locals_ = [
        pltpu.make_async_copy(shards[a], wides[a].at[own], local_sem.at[a])
        for a in range(n_arrays)
    ]
    for copy in locals_:
        copy.start()
    for a in range(n_arrays):
        send_plane(a)
        if a + 2 < n_arrays:
            send_line(a + 2)
        if a:
            send_pair(a - 1)
    send_pair(n_arrays - 1)
    for a in range(n_arrays):
        finish(a)
    for copy in locals_:
        copy.wait()


def gather_blocks(blocks):
    n_replica, n_shard = lax.axis_size("replica"), lax.axis_size("shard")
    n_arrays = len(blocks)
    n_chips = n_replica // 2
    dma = pltpu.SemaphoreType.DMA
    return pl.pallas_call(
        functools.partial(gather_kernel, n_replica, n_shard, n_arrays),
        out_shape=[
            jax.ShapeDtypeStruct((n_shard,) + block.shape, block.dtype) for block in blocks
        ],
        in_specs=[pl.BlockSpec(memory_space=pl.ANY)] * n_arrays,
        out_specs=[pl.BlockSpec(memory_space=pl.ANY)] * n_arrays,
        scratch_shapes=[
            dma((n_arrays,)),
            dma((n_arrays, n_shard - 1)),
            dma((n_arrays, n_shard - 1, n_chips - 1)),
            dma((n_arrays, n_shard - 1, n_chips)),
            dma((n_arrays, n_shard, n_replica)),
        ],
        compiler_params=pltpu.CompilerParams(collective_id=0, has_side_effects=True),
    )(*blocks)


def gather_weights(norm_one, norm_two, qkv_weight, output_weight, gate_weight, up_weight, down_weight):
    own_rows, width = output_weight.shape

    def padded(block, extra):
        rows = -(-(block.shape[0] + extra) // UNIT) * UNIT
        return jnp.pad(block, ((0, rows - block.shape[0]), (0, 0)))

    gains = jnp.pad(jnp.stack([norm_one, norm_two]), ((0, 0), (0, width - own_rows)))
    mixed_block = padded(jnp.concatenate([output_weight, gains]), 0)
    blocks = [mixed_block] + [
        padded(block, 0) for block in (qkv_weight, gate_weight, up_weight, down_weight)
    ]
    wide_mixed, *wides = gather_blocks(blocks)
    gain_one = wide_mixed[:, own_rows, :own_rows].reshape(-1)
    gain_two = wide_mixed[:, own_rows + 1, :own_rows].reshape(-1)

    def whole(wide, rows):
        return wide[:, :rows].reshape(-1, wide.shape[-1])

    return (
        gain_one,
        gain_two,
        whole(wides[0], own_rows),
        whole(wide_mixed, own_rows),
        whole(wides[1], own_rows),
        whole(wides[2], own_rows),
        whole(wides[3], down_weight.shape[0]),
    )


def over_copies(rows):
    return lax.all_gather(rows, "replica", axis=0, tiled=True)


def exchange_columns(members):
    n_replica = lax.axis_size("replica")
    count = members[0].shape[0]
    columns = jnp.concatenate(
        [member.reshape(count, n_replica, -1) for member in members], axis=2
    )
    columns = lax.all_to_all(columns, "replica", split_axis=1, concat_axis=0, tiled=True)
    return columns.reshape(n_replica * count, -1)


def sum_over_shard(part, n_rows):
    n_shard = lax.axis_size("shard")
    terms = lax.all_to_all(
        part.astype(jnp.bfloat16).reshape(n_shard, n_rows, -1),
        "shard",
        split_axis=0,
        concat_axis=0,
        tiled=True,
    )
    return jnp.sum(terms.astype(jnp.float32), axis=0).astype(jnp.bfloat16)


def feed_grads(normed_two, normed_two_all, out_grad_all, gate_back, up_back, act):
    n_replica = lax.axis_size("replica")
    n_shard = lax.axis_size("shard")
    count, width = normed_two.shape
    ff_part = act.shape[1] // n_replica
    act_parts = act.reshape(count, n_shard, n_replica, -1).swapaxes(1, 2)
    columns = exchange_columns([gate_back, up_back, act_parts])
    row_part = matmul_left_t(normed_two_all, columns[:, : 2 * ff_part])
    down_part = matmul_left_t(columns[:, 2 * ff_part :], out_grad_all)
    row_all = lax.all_gather(sum_over_shard(row_part, width // n_shard), "replica", axis=0)
    down_all = over_copies(sum_over_shard(down_part, ff_part // n_shard))
    return row_all, down_all.astype(jnp.float32)


def attention_grads(normed_one_all, context_all, qkv_back, attn_low):
    n_replica = lax.axis_size("replica")
    n_shard = lax.axis_size("shard")
    width = normed_one_all.shape[1]
    qkv_part = qkv_back.shape[1] // n_replica
    columns = exchange_columns([qkv_back, attn_low])
    row_part = jnp.concatenate(
        [
            matmul_left_t(normed_one_all, columns[:, :qkv_part]),
            matmul_left_t(context_all, columns[:, qkv_part:]),
        ],
        axis=1,
    )
    return lax.all_gather(sum_over_shard(row_part, width // n_shard), "replica", axis=0)


def unpack_kernel(widths, feed_ref, attn_ref, *out_refs):
    n_replica = feed_ref.shape[0]
    query_ref, key_ref, value_ref, output_ref, gate_ref, up_ref = out_refs
    feed = [feed_ref[part].astype(jnp.float32) for part in range(n_replica)]
    attn = [attn_ref[part].astype(jnp.float32) for part in range(n_replica)]
    ff_part = feed[0].shape[1] // 2
    qkv_part = sum(widths) // n_replica
    gate_ref[...] = jnp.concatenate([piece[:, :ff_part] for piece in feed], axis=1)
    up_ref[...] = jnp.concatenate([piece[:, ff_part:] for piece in feed], axis=1)
    output_ref[...] = jnp.concatenate([piece[:, qkv_part:] for piece in attn], axis=1)
    qkv = jnp.concatenate([piece[:, :qkv_part] for piece in attn], axis=1)
    low = 0
    for ref, width in zip((query_ref, key_ref, value_ref), widths):
        ref[...] = qkv[:, low : low + width]
        low += width


def unpack(feed_all, attn_all, width, kv_width):
    n_replica, rows, feed_cols = feed_all.shape
    attn_cols = attn_all.shape[2]
    step = 48 if rows % 48 == 0 else rows
    ff = feed_cols * n_replica // 2
    out_widths = (width, kv_width, kv_width, width, ff, ff)
    return pl.pallas_call(
        functools.partial(unpack_kernel, out_widths[:3]),
        grid=(rows // step,),
        out_shape=[jax.ShapeDtypeStruct((rows, cols), jnp.float32) for cols in out_widths],
        in_specs=[
            pl.BlockSpec((n_replica, step, feed_cols), lambda i: (0, i, 0)),
            pl.BlockSpec((n_replica, step, attn_cols), lambda i: (0, i, 0)),
        ],
        out_specs=[pl.BlockSpec((step, cols), lambda i: (i, 0)) for cols in out_widths],
        compiler_params=pltpu.CompilerParams(vmem_limit_bytes=32 * 1024 * 1024),
    )(feed_all, attn_all)


def on_device(
    tokens,
    seq_lengths,
    norm_one,
    query_weight,
    key_weight,
    value_weight,
    output_weight,
    norm_two,
    gate_weight,
    up_weight,
    down_weight,
    out_grad,
):
    count, width = tokens.shape
    group_heads = HEADS // KV_HEADS
    score_scale = 1.0 / math.sqrt(HEAD)
    doc_index, positions = layout(seq_lengths[0], count)
    cosine, sine = tables(positions, HEAD)
    slots = jnp.arange(count, dtype=jnp.int32)
    allowed = (doc_index[:, None] == doc_index[None, :]) & (slots[:, None] >= slots[None, :])
    gain_one, gain_two, wide_qkv, wide_output, wide_gate, wide_up, wide_down = gather_weights(
        norm_one,
        norm_two,
        jnp.concatenate([query_weight, key_weight, value_weight], axis=1),
        output_weight,
        gate_weight,
        up_weight,
        down_weight,
    )
    hidden_in = tokens.astype(jnp.float32)
    scale_one = lax.rsqrt(jnp.mean(hidden_in * hidden_in, axis=-1, keepdims=True) + EPSILON)
    normed_one = (hidden_in * scale_one * gain_one.astype(jnp.float32)).astype(jnp.bfloat16)
    qkv_pre = matmul(normed_one, wide_qkv)
    kv_width = KV_HEADS * HEAD
    queries_pre = qkv_pre[:, :width].reshape(count, HEADS, HEAD)
    query_rot = (
        rotate(queries_pre, cosine, sine)
        .astype(jnp.bfloat16)
        .reshape(count, KV_HEADS, group_heads, HEAD)
    )
    keys_pre = qkv_pre[:, width : width + kv_width].reshape(count, KV_HEADS, HEAD)
    key_rot = rotate(keys_pre, cosine, sine).astype(jnp.bfloat16)
    value_rot = qkv_pre[:, width + kv_width :].astype(jnp.bfloat16).reshape(count, KV_HEADS, HEAD)
    scores = masked_scores(query_rot, key_rot, allowed, score_scale)
    log_total = jax.nn.logsumexp(scores, axis=-1, keepdims=True)
    probs_low = jnp.exp(scores - log_total).astype(jnp.bfloat16)
    context = jnp.einsum("khts,skd->tkhd", probs_low, value_rot, preferred_element_type=jnp.float32)
    context = context.reshape(count, width).astype(jnp.bfloat16)
    after_attn = hidden_in + matmul(context, wide_output)
    scale_two = lax.rsqrt(jnp.mean(after_attn * after_attn, axis=-1, keepdims=True) + EPSILON)
    normed_two = (after_attn * scale_two * gain_two.astype(jnp.float32)).astype(jnp.bfloat16)
    rows_all = lax.all_gather(jnp.stack([normed_one, context, normed_two]), "replica", axis=0)
    normed_one_all, context_all, normed_two_all = (
        rows_all[:, member].reshape(-1, width) for member in range(3)
    )
    gate_pre = matmul(normed_two, wide_gate)
    up_pre = matmul(normed_two, wide_up)
    sigmoid_gate = jax.nn.sigmoid(gate_pre)
    silu_gate = gate_pre * sigmoid_gate
    act = (silu_gate * up_pre).astype(jnp.bfloat16)
    mixed = (after_attn + matmul(act, wide_down)).astype(jnp.bfloat16)
    cotangent = out_grad.astype(jnp.float32)
    act_grad = matmul_right_t(out_grad, wide_down)
    gate_back = (act_grad * up_pre * sigmoid_gate * (1.0 + gate_pre * (1.0 - sigmoid_gate))).astype(
        jnp.bfloat16
    )
    up_back = (act_grad * silu_gate).astype(jnp.bfloat16)
    normed_two_grad = matmul_right_t(gate_back, wide_gate) + matmul_right_t(up_back, wide_up)
    gain_two_sum = jnp.sum(normed_two_grad * after_attn * scale_two, axis=0)
    weighted_two = normed_two_grad * gain_two.astype(jnp.float32)
    attn_out_grad = (
        cotangent
        + scale_two * weighted_two
        - after_attn * scale_two**3 * jnp.mean(after_attn * weighted_two, axis=-1, keepdims=True)
    )
    feed_all, down_grad = feed_grads(
        normed_two, normed_two_all, over_copies(out_grad), gate_back, up_back, act
    )
    attn_low = attn_out_grad.astype(jnp.bfloat16)
    context_grad = (
        matmul_right_t(attn_low, wide_output)
        .astype(jnp.bfloat16)
        .reshape(count, KV_HEADS, group_heads, HEAD)
    )
    scores = masked_scores(query_rot, key_rot, allowed, score_scale)
    probs = jnp.exp(scores - log_total)
    probs_low = probs.astype(jnp.bfloat16)
    value_back = jnp.einsum(
        "khts,tkhd->skd", probs_low, context_grad, preferred_element_type=jnp.float32
    )
    value_back = value_back.reshape(count, KV_HEADS * HEAD).astype(jnp.bfloat16)
    probs_grad = jnp.einsum(
        "tkhd,skd->khts", context_grad, value_rot, preferred_element_type=jnp.float32
    )
    row_inner = jnp.sum(probs * probs_grad, axis=-1, keepdims=True)
    score_back = (probs * (probs_grad - row_inner) * score_scale).astype(jnp.bfloat16)
    query_rot_grad = jnp.einsum(
        "khts,skd->tkhd", score_back, key_rot, preferred_element_type=jnp.float32
    )
    key_rot_grad = jnp.einsum(
        "khts,tkhd->skd", score_back, query_rot, preferred_element_type=jnp.float32
    )
    query_back = (
        unrotate(query_rot_grad.reshape(count, HEADS, HEAD), cosine, sine)
        .reshape(count, width)
        .astype(jnp.bfloat16)
    )
    key_back = (
        unrotate(key_rot_grad, cosine, sine).reshape(count, KV_HEADS * HEAD).astype(jnp.bfloat16)
    )
    qkv_back = jnp.concatenate([query_back, key_back, value_back], axis=1)
    normed_one_grad = matmul_right_t(qkv_back, wide_qkv)
    gain_one_sum = jnp.sum(normed_one_grad * hidden_in * scale_one, axis=0)
    weighted_one = normed_one_grad * gain_one.astype(jnp.float32)
    input_grad = (
        attn_out_grad
        + scale_one * weighted_one
        - hidden_in * scale_one**3 * jnp.mean(hidden_in * weighted_one, axis=-1, keepdims=True)
    )
    gain_sums = lax.psum(jnp.stack([gain_one_sum, gain_two_sum]), ("replica", "shard"))
    own_rows = width // lax.axis_size("shard")
    gain_own = lax.dynamic_slice_in_dim(
        gain_sums, lax.axis_index("shard") * own_rows, own_rows, axis=1
    )
    attn_all = attention_grads(normed_one_all, context_all, qkv_back, attn_low)
    grads = unpack(feed_all, attn_all, width, kv_width)
    return (
        mixed,
        input_grad,
        gain_own[0],
        grads[0],
        grads[1],
        grads[2],
        grads[3],
        gain_own[1],
        grads[4],
        grads[5],
        down_grad,
    )


def solution(mesh):
    in_specs = (
        P(("replica", "shard"), None),
        P(("replica", "shard"), None),
        P("shard"),
        P("shard", None),
        P("shard", None),
        P("shard", None),
        P("shard", None),
        P("shard"),
        P("shard", None),
        P("shard", None),
        P("shard", None),
        P(("replica", "shard"), None),
    )
    out_specs = (
        P(("replica", "shard"), None),
        P(("replica", "shard"), None),
        P("shard"),
        P("shard", None),
        P("shard", None),
        P("shard", None),
        P("shard", None),
        P("shard"),
        P("shard", None),
        P("shard", None),
        P("shard", None),
    )
    return jax.shard_map(
        on_device, mesh=mesh, in_specs=in_specs, out_specs=out_specs, check_vma=False
    )
```
